512 devices in a mesh: row: 32 (over x_lo, z, core), col: 16 (over y, x_hi).
Axes of the slice: x: 4 (x_hi: 2, x_lo: 2; x = x_hi * 2 + x_lo), y: 8, z: 8, core: 2. Of those that a mesh axis runs over, the one named last changes fastest.
Arguments:
- inputs: bfloat16 [4096, 8192], P('col', 'row'), may hold values from -4 to 4
- out_grad: bfloat16 [4096, 10240], P('row', 'col'), may hold values from -6 to 6
- weight: bfloat16 [8192, 10240], P('row', 'col'), may hold values from -0.0625 to 0.0625
Outputs:
- w_grad: float32 [8192, 10240], P('row', 'col')
- input_grad: bfloat16 [4096, 8192], P('col', 'row')
The draws below stay inside these ranges and needn't reach their ends.
All inputs are finite; a program needn't handle non-finite values.
Results may differ from the reference program's by a relative error of at most 0.019.
Values may be sent and summed in bfloat16 or wider, within the bound.
No kernel may reach another device: no remote copies, remote signals or barrier semaphores. Data moves between devices by JAX's collectives and lax.ppermute only.
A program may use at most 64 MiB of HBM per device.

```python
import jax
import jax.numpy as jnp
from jax import lax

D = 8192
E = 10240
TOKENS = 4096
N_COL = 16


def strengthened(result, key, source, target, blocks, factor):
    def block_of(dim):
        return (jnp.arange(result.shape[dim]) // (result.shape[dim] // blocks)).reshape((-1,) + (1,) * (result.ndim - 1 - dim))

    one_side = jax.random.permutation(key, blocks)[block_of(target)]
    far = (block_of(target) + blocks // 2) % blocks
    return jnp.where((block_of(source) == one_side) | (block_of(source) == far), factor * result, result)


def block_levels(own_key, shape, split, low, top_value):
    factor_of = 1.0
    for position, blocks in split:
        draws = jax.random.uniform(jax.random.fold_in(jax.random.fold_in(own_key, 6), position), (blocks,), jnp.float32, low / len(split), top_value / len(split))
        factor_of = factor_of * jnp.repeat(jnp.exp(draws), shape[position] // blocks).reshape((-1,) + (1,) * (len(shape) - 1 - position))
    return factor_of


def gaussian(stream_key, dims, deviation, most, split=(), held_as=jnp.bfloat16):
    loudness = block_levels(stream_key, dims, split, -0.22, 0.18) if split else 1.0
    values = jax.random.normal(stream_key, dims, jnp.float32) * deviation * loudness
    return jnp.minimum(jnp.maximum(values, -most), most).astype(held_as)


def bell_draw_with(rng, shape, scale, reach, pieces, heavy, kind=jnp.bfloat16):
    values = scale * jax.random.normal(rng, shape, jnp.float32)
    if pieces:
        values = values * block_levels(rng, shape, pieces, -0.22, 0.18)
    return jnp.clip(strengthened(values, jax.random.fold_in(rng, 3), *heavy), -reach, reach).astype(kind)


def setup_inputs(seed: int = 0) -> dict:
    key_of = jax.random.split(jax.random.key(seed), 4)
    return {
        "inputs": gaussian(key_of[0], (TOKENS, D), 0.3, 4.0, ((0, 16), (1, 32))),
        "out_grad": bell_draw_with(key_of[1], (TOKENS, E), 0.3, 6.0, ((0, 32), (1, 16)), (1, 0, 32, 2.75)),
        "weight": gaussian(key_of[2], (D, E), D ** -0.5, 0.0625, ((0, 32), (1, 16))),
    }


def reference(inputs, out_grad, weight):
    w_grad = lax.dot_general(inputs, out_grad, (((0,), (0,)), ((), ())), preferred_element_type=jnp.float32)
    group_width = E // N_COL

    def add_group(running, index_now):
        first = (index_now * group_width).astype(jnp.int32)
        grad_cols = lax.dynamic_slice_in_dim(out_grad, first, group_width, 1)
        weight_cols = lax.dynamic_slice_in_dim(weight, first, group_width, 1)
        partial_now = lax.dot_general(grad_cols, weight_cols, (((1,), (1,)), ((), ())), preferred_element_type=jnp.float32)
        rounded = lax.optimization_barrier(partial_now.astype(jnp.bfloat16))
        return running + rounded.astype(jnp.float32), None

    start_sum = jnp.zeros((TOKENS, D), jnp.float32)
    summed, _ = lax.scan(add_group, start_sum, jnp.arange(N_COL, dtype=jnp.int32))
    return w_grad, summed.astype(jnp.bfloat16)
```

```python
import jax
import jax.numpy as jnp
from jax import lax
from jax.sharding import Mesh, PartitionSpec as P

SWAP = ((0, 1), (1, 0))


def swap(block, axis):
    return lax.ppermute(block, axis, SWAP)


def keep_and_give(block, own, axis):
    half = block.shape[axis] // 2
    kept = lax.dynamic_slice_in_dim(block, own * half, half, axis)
    given = lax.dynamic_slice_in_dim(block, (1 - own) * half, half, axis)
    return kept, given


def in_order(own, kept, got, axis):
    return jnp.concatenate(
        [jnp.where(own == 0, kept, got), jnp.where(own == 0, got, kept)], axis=axis
    )


def ring_gather(block, axis):
    size = lax.axis_size(axis)
    me = lax.axis_index(axis)
    rows = block.shape[0]
    up = [(i, (i + 1) % size) for i in range(size)]
    down = [(i, (i - 1) % size) for i in range(size)]
    panel = jnp.zeros((size * rows,) + block.shape[1:], block.dtype)

    def put(panel, block, owner):
        return lax.dynamic_update_slice_in_dim(panel, block, lax.rem(owner + size, size) * rows, 0)

    panel = put(panel, block, me)
    rising = falling = block
    for step in range(1, size // 2 + 1):
        rising = lax.ppermute(rising, axis, up)
        panel = put(panel, rising, me - step)
        if 2 * step < size:
            falling = lax.ppermute(falling, axis, down)
            panel = put(panel, falling, me + step)
    return panel


def per_device(inputs, out_grad, weight):
    core = lax.axis_index("core")
    half = lax.axis_index("xh")

    kept, given = keep_and_give(out_grad, half, 0)
    grads = jnp.concatenate([kept, swap(given, "xh")], axis=1)
    grads, inputs, weight = lax.optimization_barrier((grads, inputs, weight))
    grads = lax.all_gather(grads, ("xl", "z"), axis=0, tiled=True)

    kept, given = keep_and_give(inputs, core, 0)
    acts = jnp.concatenate([kept, swap(given, "core")], axis=1)
    kept, given = keep_and_give(acts, half, 0)
    acts = in_order(half, kept, swap(given, "xh"), 0)
    acts = ring_gather(acts, "y")

    weights = jnp.concatenate([weight, swap(weight, "xh")], axis=1)
    weights = jnp.concatenate([weights, swap(weights, "core")], axis=0)

    grads, acts, weights = lax.optimization_barrier((grads, acts, weights))
    partial = lax.dot_general(
        grads, weights, (((1,), (1,)), ((), ())), preferred_element_type=jnp.float32
    ).astype(jnp.bfloat16)
    partial, grads, acts = lax.optimization_barrier((partial, grads, acts))
    share = lax.psum_scatter(partial, "y", scatter_dimension=0, tiled=True)
    w_part = lax.dot_general(
        acts, grads, (((0,), (0,)), ((), ())), preferred_element_type=jnp.float32
    )
    rows, columns = weight.shape
    w_part = w_part[:rows] + swap(w_part[rows:].astype(jnp.bfloat16), "core")
    w_grad = w_part[:, :columns] + swap(w_part[:, columns:].astype(jnp.bfloat16), "xh")

    share, w_grad = lax.optimization_barrier((share, w_grad))
    kept, given = keep_and_give(share, half, 0)
    share = in_order(half, kept, swap(given, "xh"), 0)
    features = share.shape[1] // 2
    input_grad = in_order(core, share[:, :features], swap(share[:, features:], "core"), 0)
    return (w_grad, input_grad)


def solution(mesh):
    rows, cols = mesh.devices.shape
    split = Mesh(
        mesh.devices.reshape(2, rows // 4, 2, cols // 2, 2), ("xl", "z", "core", "y", "xh")
    )
    row, col = ("xl", "z", "core"), ("y", "xh")
    return jax.shard_map(
        per_device,
        mesh=split,
        in_specs=(P(col, row), P(row, col), P(row, col)),
        out_specs=(P(row, col), P(col, row)),
        check_vma=False,
    )
```

```python
import jax
import jax.numpy as jnp
from jax import lax
from jax.sharding import Mesh, PartitionSpec as P

SWAP = ((0, 1), (1, 0))


def swap(block, axis):
    return lax.ppermute(block, axis, SWAP)


def in_order(own, kept, got, axis):
    return jnp.concatenate(
        [jnp.where(own == 0, kept, got), jnp.where(own == 0, got, kept)], axis=axis
    )


def exchange(pieces, axes):
    return lax.all_to_all(pieces, axes, split_axis=0, concat_axis=0, tiled=True)


def ring_gather(block, axis):
    size = lax.axis_size(axis)
    me = lax.axis_index(axis)
    up = [(i, (i + 1) % size) for i in range(size)]
    down = [(i, (i - 1) % size) for i in range(size)]
    panel = jnp.zeros((block.shape[0], size) + block.shape[2:], block.dtype)

    def put(panel, block, owner):
        return lax.dynamic_update_slice_in_dim(panel, block, lax.rem(owner + size, size), 1)

    panel = put(panel, block, me)
    rising = falling = block
    for step in range(1, size // 2 + 1):
        rising = lax.ppermute(rising, axis, up)
        panel = put(panel, rising, me - step)
        if 2 * step < size:
            falling = lax.ppermute(falling, axis, down)
            panel = put(panel, falling, me + step)
    return panel


def per_device(inputs, out_grad, weight):
    core = lax.axis_index("core")
    half = lax.axis_index("xh")
    tokens, columns = out_grad.shape
    part = tokens // 2
    features = inputs.shape[1]

    pieces = jnp.broadcast_to(out_grad.reshape(1, 2, part, columns), (2, 2, part, columns))
    pieces = exchange(pieces.reshape(4, part, columns), ("xl", "xh"))
    pieces = pieces.reshape(2, 2, part, columns)
    grads = in_order(half, pieces[:, 0], pieces[:, 1], 2)
    grads, inputs, weight = lax.optimization_barrier((grads, inputs, weight))
    grads = ring_gather(grads[:, None], "z")
    grads = grads.reshape(-1, 2 * columns)

    acts = exchange(inputs.reshape(4, part, features), ("core", "xh"))
    acts = acts.reshape(2, 2 * part, features)
    acts = jnp.concatenate([acts[0], acts[1]], axis=1)
    acts = lax.all_gather(acts, "y", axis=0, tiled=True)

    weights = jnp.concatenate([weight, swap(weight, "xh")], axis=1)
    weights = in_order(core, weights, swap(weights, "core"), 0)

    grads, weights = lax.optimization_barrier((grads, weights))
    partial = jnp.concatenate(
        [
            lax.dot_general(
                grads,
                weights[i * features : (i + 1) * features],
                (((1,), (1,)), ((), ())),
                preferred_element_type=jnp.float32,
            ).astype(jnp.bfloat16)
            for i in range(2)
        ],
        axis=0,
    )

    w_part = lax.dot_general(
        acts, grads, (((0,), (0,)), ((), ())), preferred_element_type=jnp.float32
    )
    given = lax.dynamic_slice_in_dim(w_part, (1 - core) * features, features, 0)
    kept = lax.dynamic_slice_in_dim(w_part, core * features, features, 0)
    w_part = kept + swap(given.astype(jnp.bfloat16), "core")
    kept, given = w_part[:, :columns], w_part[:, columns:].astype(jnp.bfloat16)
    kept, given, partial = lax.optimization_barrier((kept, given, partial))
    w_grad = kept + swap(given, "xh")

    partial = partial.reshape(-1, part, features)
    shares = exchange(partial, ("core", "y", "xh"))
    shares = shares.reshape(2, -1, 2, part, features).astype(jnp.float32)
    input_grad = jnp.sum(shares, axis=1).astype(jnp.bfloat16).reshape(-1, features)
    return (w_grad, input_grad)


def solution(mesh):
    rows, cols = mesh.devices.shape
    split = Mesh(
        mesh.devices.reshape(2, rows // 4, 2, cols // 2, 2), ("xl", "z", "core", "y", "xh")
    )
    row, col = ("xl", "z", "core"), ("y", "xh")
    return jax.shard_map(
        per_device,
        mesh=split,
        in_specs=(P(col, row), P(row, col), P(row, col)),
        out_specs=(P(row, col), P(col, row)),
        check_vma=False,
    )
```

```python
import jax
import jax.numpy as jnp
from jax import lax
from jax.sharding import Mesh, PartitionSpec as P

SWAP = ((0, 1), (1, 0))


def swap(block, axis):
    return lax.ppermute(block, axis, SWAP)


def in_order(own, kept, got, axis):
    return jnp.concatenate(
        [jnp.where(own == 0, kept, got), jnp.where(own == 0, got, kept)], axis=axis
    )


def keep_and_give(block, own):
    half = block.shape[0] // 2
    kept = lax.dynamic_slice_in_dim(block, own * half, half, 0)
    given = lax.dynamic_slice_in_dim(block, (1 - own) * half, half, 0)
    return kept, given


def exchange(pieces, axes):
    return lax.all_to_all(pieces, axes, split_axis=0, concat_axis=0, tiled=True)


def ring_gather(block, axis, lanes):
    size = lax.axis_size(axis)
    me = lax.axis_index(axis)
    up = [(i, (i + 1) % size) for i in range(size)]
    down = [(i, (i - 1) % size) for i in range(size)]
    panel = jnp.zeros((block.shape[0], size) + block.shape[1:], block.dtype)

    def put(panel, block, first, owner):
        at = (first, lax.rem(owner + size, size), 0, 0)
        return lax.dynamic_update_slice(panel, block[:, None], at)

    panel = put(panel, block, 0, me)
    step_rows = block.shape[0] // lanes
    rising = [block[i * step_rows : (i + 1) * step_rows] for i in range(lanes)]
    falling = list(rising)
    for step in range(1, size // 2):
        for i in range(lanes):
            rising[i] = lax.ppermute(rising[i], axis, up)
            falling[i] = lax.ppermute(falling[i], axis, down)
            panel = put(panel, rising[i], i * step_rows, me - step)
            panel = put(panel, falling[i], i * step_rows, me + step)
    rising, falling = jnp.concatenate(rising), jnp.concatenate(falling)
    middle = block.shape[0] // 2
    panel = put(panel, lax.ppermute(rising[:middle], axis, up), 0, me + size // 2)
    return put(panel, lax.ppermute(falling[middle:], axis, down), middle, me + size // 2)


def per_device(inputs, out_grad, weight):
    core = lax.axis_index("core")
    half = lax.axis_index("xh")
    tokens, columns = out_grad.shape
    part = tokens // 2
    features = inputs.shape[1]

    pieces = jnp.broadcast_to(out_grad.reshape(1, 2, part, columns), (2, 2, part, columns))
    pieces = pieces.reshape(4, part, columns)
    pieces = exchange(pieces, ("xl", "xh")).reshape(2, 2, part, columns)
    grads = in_order(half, pieces[:, 0], pieces[:, 1], 2)
    grads, inputs, weight = lax.optimization_barrier((grads, inputs, weight))
    grads = ring_gather(grads, "z", 1).reshape(-1, 2 * columns)

    kept, given = keep_and_give(inputs, core)
    acts = jnp.concatenate([kept, swap(given, "core")], axis=1)
    kept, given = keep_and_give(acts, half)
    acts = in_order(half, kept, swap(given, "xh"), 0)
    weights = in_order(core, weight, swap(weight, "core"), 0)
    acts = lax.all_gather(acts, "y", axis=0, tiled=True)
    weights = jnp.concatenate([weights, swap(weights, "xh")], axis=1)

    grads, weights = lax.optimization_barrier((grads, weights))
    partial = jnp.concatenate(
        [
            lax.dot_general(
                grads,
                weights[i * features : (i + 1) * features],
                (((1,), (1,)), ((), ())),
                preferred_element_type=jnp.float32,
            ).astype(jnp.bfloat16)
            for i in range(2)
        ],
        axis=0,
    )
    shares = exchange(partial.reshape(-1, part, features), ("core", "y", "xh"))
    shares = shares.reshape(2, -1, 2, part, features).astype(jnp.float32)
    input_grad = jnp.sum(shares, axis=1).astype(jnp.bfloat16).reshape(-1, features)

    w_part = lax.dot_general(
        acts, grads, (((0,), (0,)), ((), ())), preferred_element_type=jnp.float32
    )
    w_part = w_part[:features] + swap(w_part[features:].astype(jnp.bfloat16), "core")
    w_grad = w_part[:, :columns] + swap(w_part[:, columns:].astype(jnp.bfloat16), "xh")
    return (w_grad, input_grad)


def solution(mesh):
    rows, cols = mesh.devices.shape
    split = Mesh(
        mesh.devices.reshape(2, rows // 4, 2, cols // 2, 2), ("xl", "z", "core", "y", "xh")
    )
    row, col = ("xl", "z", "core"), ("y", "xh")
    return jax.shard_map(
        per_device,
        mesh=split,
        in_specs=(P(col, row), P(row, col), P(row, col)),
        out_specs=(P(row, col), P(col, row)),
        check_vma=False,
    )
```

```python
import functools

import jax
import jax.numpy as jnp
from jax import lax
from jax.experimental import pallas as pl
from jax.experimental.pallas import tpu as pltpu
from jax.sharding import Mesh, PartitionSpec as P


def swap(block, axis):
    return lax.ppermute(block, axis, ((0, 1), (1, 0)))


def in_order(own, kept, got, axis):
    return jnp.concatenate(
        [jnp.where(own == 0, kept, got), jnp.where(own == 0, got, kept)], axis=axis
    )


def pick(block, index, axis):
    return lax.dynamic_slice_in_dim(block, index, 1, axis)


def exchange(pieces, axes):
    return lax.all_to_all(pieces, axes, split_axis=0, concat_axis=0, tiled=True)


def times(left, right, left_dims, right_dims):
    return lax.dot_general(
        left, right, ((left_dims, right_dims), ((), ())), preferred_element_type=jnp.float32
    )


def project_kernel(part, own_ref, other_ref, weight_ref, out_ref):
    features = out_ref.shape[-1]
    for c, g in enumerate((own_ref, other_ref)):
        for i in range(2):
            w = weight_ref.at[:, i * features : (i + 1) * features]
            acc = times(g[0], w[0], (1,), (1,)) + times(g[1], w[1], (1,), (1,))
            acc = acc.reshape(-1, part, features)
            out_ref[i, :, c * part : (c + 1) * part, :] = acc.astype(out_ref.dtype)


def project(own, other, weights, part):
    _, rows, columns = own.shape
    features = weights.shape[1] // 2
    blocks = rows // part
    steps = 4
    grads_spec = pl.BlockSpec((2, rows // steps, columns), lambda r: (0, r, 0))
    return pl.pallas_call(
        functools.partial(project_kernel, part),
        out_shape=jax.ShapeDtypeStruct((2, blocks, 2 * part, features), own.dtype),
        grid=(steps,),
        in_specs=[grads_spec, grads_spec, pl.BlockSpec(weights.shape, lambda r: (0, 0, 0))],
        out_specs=pl.BlockSpec(
            (2, blocks // steps, 2 * part, features), lambda r: (0, r, 0, 0)
        ),
        compiler_params=pltpu.CompilerParams(vmem_limit_bytes=24 * 2**20),
        cost_estimate=pl.CostEstimate(
            flops=8 * rows * columns * 2 * features,
            bytes_accessed=2 * (2 * own.size + weights.size + 4 * rows * features),
            transcendentals=0,
        ),
    )(own, other, weights)


def per_device(inputs, out_grad, weight):
    core = lax.axis_index("core")
    near = lax.axis_index("xl")
    far = lax.axis_index("xh")
    depth = lax.axis_size("z")
    tokens, columns = out_grad.shape
    features = inputs.shape[1]
    part = tokens // 4

    grads = jnp.broadcast_to(
        out_grad.reshape(2, 2, part, columns).transpose(1, 0, 2, 3)[:, :, None],
        (2, 2, depth, part, columns),
    ).reshape(-1, part, columns)
    grads = exchange(grads, ("xh", "xl", "z")).reshape(2, -1, columns)

    acts = inputs.reshape(2, 2, 2, part, features)
    acts = jnp.concatenate(
        [pick(acts, near, 1), swap(pick(acts, 1 - near, 1), "xl")], axis=4
    )
    acts = in_order(far, pick(acts, far, 2), swap(pick(acts, 1 - far, 2), "xh"), 2)
    acts = jnp.concatenate([pick(acts, core, 0), pick(acts, 1 - core, 0)], axis=0)
    acts = acts.reshape(4 * part, 2 * features)
    weights = in_order(far, weight[None], swap(weight, "xh")[None], 0)
    weights, acts = lax.optimization_barrier((weights, acts))
    weights = in_order(near, weights, swap(weights, "xl"), 1)

    acts = lax.all_gather(acts, "y", axis=0, tiled=True)
    grads, weights = lax.optimization_barrier((grads, weights))
    others = swap(grads, "core")

    partial = project(grads, others, weights, part)
    shares = exchange(partial.reshape(-1, 2 * part, features), ("xl", "y", "xh"))
    shares = shares.reshape(2, -1, 2, 2, part, features).astype(jnp.float32)
    shares = jnp.sum(shares, axis=1).astype(jnp.bfloat16)
    shares = shares.transpose(2, 0, 1, 3, 4)
    shares = in_order(core, shares[:1], shares[1:], 0)
    input_grad = shares.reshape(-1, features)

    acts = acts.reshape(-1, 2, 2 * part, 2 * features)
    w_part = sum(
        times(acts[:, i].reshape(-1, 2 * features), g, (0,), (1,))
        for i, g in enumerate((grads, others))
    )
    w_part = w_part.reshape(2, features, 2, columns)

    def piece(a, b):
        return pick(pick(w_part, a, 0), b, 2).reshape(features, columns)

    w_grad = piece(0, far)
    for a, b in ((1, 0), (0, 1), (1, 1)):
        perm = [(i, i ^ (2 * a + b)) for i in range(4)]
        sent = piece(a, far ^ b).astype(jnp.bfloat16)
        w_grad = w_grad + lax.ppermute(sent, ("xl", "xh"), perm)
    return (w_grad, input_grad)


def solution(mesh):
    rows, cols = mesh.devices.shape
    split = Mesh(
        mesh.devices.reshape(2, rows // 4, 2, cols // 2, 2), ("xl", "z", "core", "y", "xh")
    )
    row, col = ("xl", "z", "core"), ("y", "xh")
    return jax.shard_map(
        per_device,
        mesh=split,
        in_specs=(P(col, row), P(row, col), P(row, col)),
        out_specs=(P(row, col), P(col, row)),
        check_vma=False,
    )
```

```python
import jax
import jax.numpy as jnp
from jax import lax
from jax.sharding import Mesh, PartitionSpec as P

PAIRS = ((1, 0), (0, 1), (1, 1))


def swap(block, axis):
    return lax.ppermute(block, axis, ((0, 1), (1, 0)))


def to_partner(block, a, b):
    return lax.ppermute(block, ("xl", "xh"), [(i, i ^ (2 * a + b)) for i in range(4)])


def in_order(own, kept, got, axis):
    return jnp.concatenate(
        [jnp.where(own == 0, kept, got), jnp.where(own == 0, got, kept)], axis=axis
    )


def pick(block, index, axis):
    return lax.dynamic_slice_in_dim(block, index, 1, axis)


def exchange(pieces, axes):
    return lax.all_to_all(pieces, axes, split_axis=0, concat_axis=0, tiled=True)


def times(left, right, left_dim, right_dim):
    return lax.dot_general(
        left,
        right,
        (((left_dim,), (right_dim,)), ((), ())),
        preferred_element_type=jnp.float32,
    )


def per_device(inputs, out_grad, weight):
    core = lax.axis_index("core")
    near = lax.axis_index("xl")
    far = lax.axis_index("xh")
    depth = lax.axis_size("z")
    tokens, columns = out_grad.shape
    features = inputs.shape[1]
    part = tokens // 4

    grads = jnp.broadcast_to(
        out_grad.reshape(4, 1, part, columns), (4, depth, part, columns)
    ).reshape(-1, part, columns)
    grads = exchange(grads, ("xl", "xh", "z"))

    acts = lax.all_gather(inputs, "y", axis=0, tiled=False)

    came = {(a, b): to_partner(weight, a, b) for a, b in PAIRS}
    came[0, 0] = weight
    weights = [in_order(far, came[a, 0], came[a, 1], 1) for a in range(2)]
    weights = in_order(near, weights[0], weights[1], 0)
    grads, weights, acts = lax.optimization_barrier((grads, weights, acts))

    acts = acts.reshape(-1, 2, 4, part, features)

    def quarter(a, b):
        rows = pick(acts, 2 * (near ^ a) + (far ^ b), 2)
        rows = jnp.concatenate([pick(rows, core, 1), pick(rows, 1 - core, 1)], axis=1)
        return rows.reshape(-1, 2 * part, features)

    came = {(a, b): to_partner(quarter(a, b), a, b) for a, b in PAIRS}
    came[0, 0] = quarter(0, 0)

    panels = [
        g.reshape(2, 2, depth, 1, part, columns) for g in (grads, swap(grads, "core"))
    ]
    panels = [jnp.concatenate([g[:, 0], g[:, 1]], axis=4) for g in panels]
    panel = jnp.concatenate(panels, axis=2).reshape(-1, 2 * columns)
    partial = [
        times(panel, weights[i * features : (i + 1) * features], 1, 1).astype(jnp.bfloat16)
        for i in range(2)
    ]
    *partial, came, panel = lax.optimization_barrier((*partial, came, panel))
    partial = jnp.concatenate(partial, axis=0).reshape(-1, 2 * part, features)
    shares = exchange(partial, ("xl", "y", "xh"))
    shares = shares.reshape(2, -1, 2, 2, part, features).astype(jnp.float32)
    shares = jnp.sum(shares, axis=1).astype(jnp.bfloat16)
    shares = shares.transpose(2, 0, 1, 3, 4)
    input_grad = in_order(core, shares[:1], shares[1:], 0).reshape(-1, features)

    acts = [jnp.concatenate([came[0, b], came[1, b]], axis=2)[:, None] for b in range(2)]
    acts = in_order(far, acts[0], acts[1], 1).reshape(-1, 2 * features)
    w_part = times(acts, panel, 0, 0)

    def piece(a, b):
        rows = w_part[a * features : (a + 1) * features]
        return lax.dynamic_slice_in_dim(rows, (far ^ b) * columns, columns, 1)

    w_grad = piece(0, 0)
    for a, b in PAIRS:
        w_grad = w_grad + to_partner(piece(a, b).astype(jnp.bfloat16), a, b)
    return (w_grad, input_grad)


def solution(mesh):
    rows, cols = mesh.devices.shape
    split = Mesh(
        mesh.devices.reshape(2, rows // 4, 2, cols // 2, 2), ("xl", "z", "core", "y", "xh")
    )
    row, col = ("xl", "z", "core"), ("y", "xh")
    return jax.shard_map(
        per_device,
        mesh=split,
        in_specs=(P(col, row), P(row, col), P(row, col)),
        out_specs=(P(row, col), P(col, row)),
        check_vma=False,
    )
```

```python
import jax
import jax.numpy as jnp
from jax import lax
from jax.sharding import Mesh, PartitionSpec as P

SWAP = ((0, 1), (1, 0))


def swap(block, axis):
    return lax.ppermute(block, axis, SWAP)


def in_order(own, kept, got, axis):
    return jnp.concatenate(
        [jnp.where(own == 0, kept, got), jnp.where(own == 0, got, kept)], axis=axis
    )


def exchange(pieces, axes):
    return lax.all_to_all(pieces, axes, split_axis=0, concat_axis=0, tiled=True)


def ring_gather(block, axis, lanes):
    size = lax.axis_size(axis)
    me = lax.axis_index(axis)
    up = [(i, (i + 1) % size) for i in range(size)]
    down = [(i, (i - 1) % size) for i in range(size)]
    panel = jnp.zeros((block.shape[0], size) + block.shape[1:], block.dtype)

    def put(panel, block, first, owner):
        at = (first, lax.rem(owner + size, size), 0, 0)
        return lax.dynamic_update_slice(panel, block[:, None], at)

    panel = put(panel, block, 0, me)
    step_rows = block.shape[0] // lanes
    rising = [block[i * step_rows : (i + 1) * step_rows] for i in range(lanes)]
    falling = list(rising)
    for step in range(1, size // 2):
        for i in range(lanes):
            rising[i] = lax.ppermute(rising[i], axis, up)
            falling[i] = lax.ppermute(falling[i], axis, down)
            panel = put(panel, rising[i], i * step_rows, me - step)
            panel = put(panel, falling[i], i * step_rows, me + step)
    rising, falling = jnp.concatenate(rising), jnp.concatenate(falling)
    middle = block.shape[0] // 2
    panel = put(panel, lax.ppermute(rising[:middle], axis, up), 0, me + size // 2)
    return put(panel, lax.ppermute(falling[middle:], axis, down), middle, me + size // 2)


def per_device(inputs, out_grad, weight):
    core = lax.axis_index("core")
    half = lax.axis_index("xh")
    tokens, columns = out_grad.shape
    part = tokens // 2
    features = inputs.shape[1]

    pieces = jnp.broadcast_to(out_grad.reshape(1, 2, part, columns), (2, 2, part, columns))
    pieces = exchange(pieces.reshape(4, part, columns), ("xl", "xh"))

    quarters = inputs.reshape(4, part, features)

    def quarter(a, b):
        return lax.dynamic_index_in_dim(quarters, 2 * (core ^ a) + (half ^ b), 0, False)

    came = {}
    for a, b in ((1, 0), (0, 1), (1, 1)):
        partner = [(i, i ^ (2 * a + b)) for i in range(4)]
        came[a, b] = lax.ppermute(quarter(a, b), ("core", "xh"), partner)
    came[0, 0] = quarter(0, 0)
    pieces, came, weight = lax.optimization_barrier((pieces, came, weight))
    pieces = pieces.reshape(2, 2, part, columns)
    grads = in_order(half, pieces[:, 0], pieces[:, 1], 2)
    acts = [jnp.concatenate([came[0, b], came[1, b]], axis=1) for b in range(2)]
    acts = in_order(half, acts[0], acts[1], 0)
    grads, acts, weight = lax.optimization_barrier((grads, acts, weight))
    grads = ring_gather(grads, "z", 1).reshape(-1, 2 * columns)
    acts = lax.all_gather(acts, "y", axis=0, tiled=True)

    weights = in_order(core, weight, swap(weight, "core"), 0)
    weights = jnp.concatenate([weights, swap(weights, "xh")], axis=1)

    grads, weights = lax.optimization_barrier((grads, weights))
    partial = jnp.concatenate(
        [
            lax.dot_general(
                grads,
                weights[i * features : (i + 1) * features],
                (((1,), (1,)), ((), ())),
                preferred_element_type=jnp.float32,
            ).astype(jnp.bfloat16)
            for i in range(2)
        ],
        axis=0,
    )
    shares = exchange(partial.reshape(-1, part, features), ("core", "y", "xh"))
    shares = shares.reshape(2, -1, 2, part, features).astype(jnp.float32)
    input_grad = jnp.sum(shares, axis=1).astype(jnp.bfloat16).reshape(-1, features)

    w_part = lax.dot_general(
        acts, grads, (((0,), (0,)), ((), ())), preferred_element_type=jnp.float32
    )
    w_part = w_part[:features] + swap(w_part[features:].astype(jnp.bfloat16), "core")
    w_grad = w_part[:, :columns] + swap(w_part[:, columns:].astype(jnp.bfloat16), "xh")
    return (w_grad, input_grad)


def solution(mesh):
    rows, cols = mesh.devices.shape
    split = Mesh(
        mesh.devices.reshape(2, rows // 4, 2, cols // 2, 2), ("xl", "z", "core", "y", "xh")
    )
    row, col = ("xl", "z", "core"), ("y", "xh")
    return jax.shard_map(
        per_device,
        mesh=split,
        in_specs=(P(col, row), P(row, col), P(row, col)),
        out_specs=(P(row, col), P(col, row)),
        check_vma=False,
    )
```

```python
import jax
import jax.numpy as jnp
from jax import lax
from jax.sharding import Mesh, PartitionSpec as P

SWAP = ((0, 1), (1, 0))


def swap(block, axis):
    return lax.ppermute(block, axis, SWAP)


def in_order(own, kept, got, axis):
    return jnp.concatenate(
        [jnp.where(own == 0, kept, got), jnp.where(own == 0, got, kept)], axis=axis
    )


def pick(block, index, axis):
    return lax.dynamic_slice_in_dim(block, index, 1, axis)


def exchange(pieces, axes):
    return lax.all_to_all(pieces, axes, split_axis=0, concat_axis=0, tiled=True)


def ring_gather(block, weights):
    core = lax.axis_index("core")
    me = lax.axis_index("z")
    size = lax.axis_size("z")
    sign = 1 - 2 * core
    one_way = [
        (2 * i + c, 2 * ((i + 1 - 2 * c) % size) + c) for i in range(size) for c in range(2)
    ]
    other_way = [(target, source) for source, target in one_way]
    panel = jnp.zeros((block.shape[0], size) + block.shape[1:], block.dtype)

    def put(panel, block, first, steps):
        at = (first, lax.rem(me - sign * steps + size, size), 0, 0)
        return lax.dynamic_update_slice(panel, block[:, None], at)

    panel = put(panel, block, 0, 0)
    one = two = block
    for step in range(1, size // 2):
        one = lax.ppermute(one, ("z", "core"), one_way)
        two = lax.ppermute(two, ("z", "core"), other_way)
        panel = put(panel, one, 0, step)
        panel = put(panel, two, 0, -step)
        if step == min(2, size // 2 - 1):
            one, weights = lax.optimization_barrier((one, weights))
            weights = in_order(core, weights, swap(weights, "core"), 0)
    middle = block.shape[0] // 2
    one = lax.ppermute(one[:middle], ("z", "core"), one_way)
    two = lax.ppermute(two[middle:], ("z", "core"), other_way)
    panel = put(panel, one, 0, size // 2)
    return put(panel, two, middle, size // 2), weights


def per_device(inputs, out_grad, weight):
    core = lax.axis_index("core")
    half = lax.axis_index("xh")
    tokens, columns = out_grad.shape
    part = tokens // 2
    features = inputs.shape[1]

    pieces = jnp.broadcast_to(out_grad.reshape(1, 2, part, columns), (2, 2, part, columns))
    pieces = pieces.reshape(4, part, columns)
    pieces = exchange(pieces, ("xl", "xh"))
    acts = inputs.reshape(2, 2, part, features)
    acts = in_order(half, pick(acts, half, 1), swap(pick(acts, 1 - half, 1), "xh"), 1)
    pieces, acts, weight = lax.optimization_barrier((pieces, acts, weight))
    acts = jnp.concatenate([pick(acts, core, 0), pick(acts, 1 - core, 0)], axis=0)
    acts = lax.all_gather(acts.reshape(2, 2 * part, features), "y", axis=0, tiled=False)

    pieces = pieces.reshape(2, 2, part, columns)
    grads = in_order(half, pieces[:, 0], pieces[:, 1], 2)
    grads, weight = lax.optimization_barrier((grads, weight))
    weights = jnp.concatenate([weight, swap(weight, "xh")], axis=1)
    grads, weights = ring_gather(grads, weights)
    grads = grads.reshape(-1, 2 * columns)

    grads, weights = lax.optimization_barrier((grads, weights))
    partial = [
        lax.dot_general(
            grads,
            weights[i * features : (i + 1) * features],
            (((1,), (1,)), ((), ())),
            preferred_element_type=jnp.float32,
        ).astype(jnp.bfloat16)
        for i in range(2)
    ]
    got = swap(acts[:, 1], "core")
    *partial, got, grads = lax.optimization_barrier((*partial, got, grads))
    acts = jnp.concatenate([acts[:, 0], got], axis=2).reshape(-1, 2 * features)

    partial = jnp.concatenate(partial, axis=0)
    shares = exchange(partial.reshape(-1, part, features), ("core", "y", "xh"))
    shares = shares.reshape(2, -1, 2, part, features).astype(jnp.float32)
    input_grad = jnp.sum(shares, axis=1).astype(jnp.bfloat16).reshape(-1, features)

    w_part = lax.dot_general(
        acts, grads, (((0,), (0,)), ((), ())), preferred_element_type=jnp.float32
    )
    w_part = w_part[:features] + swap(w_part[features:].astype(jnp.bfloat16), "core")
    w_grad = w_part[:, :columns] + swap(w_part[:, columns:].astype(jnp.bfloat16), "xh")
    return (w_grad, input_grad)


def solution(mesh):
    rows, cols = mesh.devices.shape
    split = Mesh(
        mesh.devices.reshape(2, rows // 4, 2, cols // 2, 2), ("xl", "z", "core", "y", "xh")
    )
    row, col = ("xl", "z", "core"), ("y", "xh")
    return jax.shard_map(
        per_device,
        mesh=split,
        in_specs=(P(col, row), P(row, col), P(row, col)),
        out_specs=(P(row, col), P(col, row)),
        check_vma=False,
    )
```

```python
import jax
import jax.numpy as jnp
from jax import lax
from jax.sharding import Mesh, PartitionSpec as P

PAIRS = ((1, 0), (0, 1), (1, 1))


def swap(block, axis):
    return lax.ppermute(block, axis, ((0, 1), (1, 0)))


def to_partner(block, a, b):
    return lax.ppermute(block, ("xl", "xh"), [(i, i ^ (2 * a + b)) for i in range(4)])


def in_order(own, kept, got, axis):
    return jnp.concatenate(
        [jnp.where(own == 0, kept, got), jnp.where(own == 0, got, kept)], axis=axis
    )


def pick(block, index, axis):
    return lax.dynamic_slice_in_dim(block, index, 1, axis)


def exchange(pieces, axes):
    return lax.all_to_all(pieces, axes, split_axis=0, concat_axis=0, tiled=True)


def times(left, right, left_dim, right_dim):
    return lax.dot_general(
        left,
        right,
        (((left_dim,), (right_dim,)), ((), ())),
        preferred_element_type=jnp.float32,
    )


def ring_gather(block, axis):
    size = lax.axis_size(axis)
    me = lax.axis_index(axis)
    rows = block.shape[0]
    up = [(i, (i + 1) % size) for i in range(size)]
    down = [(i, (i - 1) % size) for i in range(size)]
    panel = jnp.zeros((size * rows,) + block.shape[1:], block.dtype)

    def put(panel, block, owner, first):
        at = lax.rem(owner + size, size) * rows + first
        return lax.dynamic_update_slice_in_dim(panel, block, at, 0)

    panel = put(panel, block, me, 0)
    rising = falling = block
    for step in range(1, size // 2):
        rising = lax.ppermute(rising, axis, up)
        falling = lax.ppermute(falling, axis, down)
        panel = put(panel, rising, me - step, 0)
        panel = put(panel, falling, me + step, 0)
    rising, falling, panel = yield rising, falling, panel
    middle = rows // 2
    rising = lax.ppermute(rising[:middle], axis, up)
    falling = lax.ppermute(falling[middle:], axis, down)
    rising, falling, panel = yield rising, falling, panel
    panel = put(panel, rising, me + size // 2, 0)
    yield put(panel, falling, me + size // 2, middle)


def per_device(inputs, out_grad, weight):
    core = lax.axis_index("core")
    near = lax.axis_index("xl")
    far = lax.axis_index("xh")
    depth = lax.axis_size("z")
    tokens, columns = out_grad.shape
    features = inputs.shape[1]
    part = tokens // 4

    grads = jnp.broadcast_to(
        out_grad.reshape(4, 1, part, columns), (4, depth, part, columns)
    ).reshape(-1, part, columns)
    grads = exchange(grads, ("xl", "xh", "z"))

    acts = inputs.reshape(2, 4, part, features)
    acts = jnp.concatenate([pick(acts, core, 0), pick(acts, 1 - core, 0)], axis=0)

    def quarter(a, b):
        return pick(acts, 2 * (near ^ a) + (far ^ b), 1).reshape(1, 2, part, features)

    came = {(a, b): to_partner(quarter(a, b), a, b) for a, b in PAIRS}
    came[0, 0] = quarter(0, 0)
    rows = [jnp.concatenate([came[0, b], came[1, b]], axis=3) for b in range(2)]
    acts = in_order(far, rows[0], rows[1], 0).reshape(4 * part, 2 * features)
    acts, weight = lax.optimization_barrier((acts, weight))

    came = {(a, b): to_partner(weight, a, b) for a, b in PAIRS}
    came[0, 0] = weight
    weights = [in_order(far, came[a, 0], came[a, 1], 1) for a in range(2)]
    weights = in_order(near, weights[0], weights[1], 0)
    gather = ring_gather(acts, "y")
    ring = next(gather)
    grads, weights, *ring = lax.optimization_barrier((grads, weights, *ring))
    ring = gather.send(ring)

    panels = [
        g.reshape(2, 2, depth, 1, part, columns) for g in (grads, swap(grads, "core"))
    ]
    panels = [jnp.concatenate([g[:, 0], g[:, 1]], axis=4) for g in panels]
    panel = jnp.concatenate(panels, axis=2).reshape(-1, 2 * columns)
    partial = [
        times(panel, weights[i * features : (i + 1) * features], 1, 1).astype(jnp.bfloat16)
        for i in range(2)
    ]
    *partial, panel, ring = lax.optimization_barrier((*partial, panel, ring))
    acts = gather.send(ring)
    partial = jnp.concatenate(partial, axis=0).reshape(-1, 2 * part, features)
    shares = exchange(partial, ("xl", "y", "xh"))
    shares = shares.reshape(2, -1, 2, 2, part, features).astype(jnp.float32)
    shares = jnp.sum(shares, axis=1).astype(jnp.bfloat16)
    shares = shares.transpose(2, 0, 1, 3, 4)
    input_grad = in_order(core, shares[:1], shares[1:], 0).reshape(-1, features)

    w_part = times(acts, panel, 0, 0)

    def piece(a, b):
        rows = w_part[a * features : (a + 1) * features]
        return lax.dynamic_slice_in_dim(rows, (far ^ b) * columns, columns, 1)

    w_grad = piece(0, 0)
    for a, b in PAIRS:
        w_grad = w_grad + to_partner(piece(a, b).astype(jnp.bfloat16), a, b)
    return (w_grad, input_grad)


def solution(mesh):
    rows, cols = mesh.devices.shape
    split = Mesh(
        mesh.devices.reshape(2, rows // 4, 2, cols // 2, 2), ("xl", "z", "core", "y", "xh")
    )
    row, col = ("xl", "z", "core"), ("y", "xh")
    return jax.shard_map(
        per_device,
        mesh=split,
        in_specs=(P(col, row), P(row, col), P(row, col)),
        out_specs=(P(row, col), P(col, row)),
        check_vma=False,
    )
```

```python
import jax
import jax.numpy as jnp
from jax import lax
from jax.sharding import Mesh, PartitionSpec as P

PAIRS = ((1, 0), (0, 1), (1, 1))


def swap(block, axis):
    return lax.ppermute(block, axis, ((0, 1), (1, 0)))


def to_partner(block, a, b):
    return lax.ppermute(block, ("xl", "xh"), [(i, i ^ (2 * a + b)) for i in range(4)])


def in_order(own, kept, got, axis):
    return jnp.concatenate(
        [jnp.where(own == 0, kept, got), jnp.where(own == 0, got, kept)], axis=axis
    )


def pick(block, index, axis):
    return lax.dynamic_slice_in_dim(block, index, 1, axis)


def exchange(pieces, axes):
    return lax.all_to_all(pieces, axes, split_axis=0, concat_axis=0, tiled=True)


def times(left, right, left_dim, right_dim):
    return lax.dot_general(
        left,
        right,
        (((left_dim,), (right_dim,)), ((), ())),
        preferred_element_type=jnp.float32,
    )


def ring_gather(block, axis):
    size = lax.axis_size(axis)
    me = lax.axis_index(axis)
    rows = block.shape[0]
    up = [(i, (i + 1) % size) for i in range(size)]
    down = [(i, (i - 1) % size) for i in range(size)]
    panel = jnp.zeros((size * rows,) + block.shape[1:], block.dtype)

    def put(panel, block, owner, first):
        at = lax.rem(owner + size, size) * rows + first
        return lax.dynamic_update_slice_in_dim(panel, block, at, 0)

    panel = put(panel, block, me, 0)
    rising = falling = block
    for step in range(1, size // 2):
        rising = lax.ppermute(rising, axis, up)
        falling = lax.ppermute(falling, axis, down)
        panel = put(panel, rising, me - step, 0)
        panel = put(panel, falling, me + step, 0)
    rising, falling, panel = yield rising, falling, panel
    middle = rows // 2
    rising = lax.ppermute(rising[:middle], axis, up)
    falling = lax.ppermute(falling[middle:], axis, down)
    rising, falling, panel = yield rising, falling, panel
    panel = put(panel, rising, me + size // 2, 0)
    yield put(panel, falling, me + size // 2, middle)


def per_device(inputs, out_grad, weight):
    core = lax.axis_index("core")
    near = lax.axis_index("xl")
    far = lax.axis_index("xh")
    depth = lax.axis_size("z")
    tokens, columns = out_grad.shape
    features = inputs.shape[1]
    part = tokens // 4

    acts = inputs.reshape(2, 4, part, features)
    acts = jnp.concatenate([pick(acts, core, 0), pick(acts, 1 - core, 0)], axis=0)

    def quarter(a, b):
        return pick(acts, 2 * (near ^ a) + (far ^ b), 1).reshape(1, 2, part, features)

    came = {(a, b): to_partner(quarter(a, b), a, b) for a, b in PAIRS}
    came[0, 0] = quarter(0, 0)
    rows = [jnp.concatenate([came[0, b], came[1, b]], axis=3) for b in range(2)]
    acts = in_order(far, rows[0], rows[1], 0).reshape(4 * part, 2 * features)
    acts, out_grad, weight = lax.optimization_barrier((acts, out_grad, weight))

    grads = jnp.broadcast_to(
        out_grad.reshape(4, 1, part, columns), (4, depth, part, columns)
    ).reshape(-1, part, columns)
    grads = exchange(grads, ("xl", "xh", "z"))

    came = {(a, b): to_partner(weight, a, b) for a, b in PAIRS}
    came[0, 0] = weight
    weights = [in_order(far, came[a, 0], came[a, 1], 1) for a in range(2)]
    weights = in_order(near, weights[0], weights[1], 0)
    gather = ring_gather(acts, "y")
    ring = next(gather)
    grads, weights, *ring = lax.optimization_barrier((grads, weights, *ring))
    ring = gather.send(ring)

    panels = [
        g.reshape(2, 2, depth, 1, part, columns) for g in (grads, swap(grads, "core"))
    ]
    panels = [jnp.concatenate([g[:, 0], g[:, 1]], axis=4) for g in panels]
    panel = jnp.concatenate(panels, axis=2).reshape(-1, 2 * columns)
    partial = [
        times(panel, weights[i * features : (i + 1) * features], 1, 1).astype(jnp.bfloat16)
        for i in range(2)
    ]
    *partial, panel, ring = lax.optimization_barrier((*partial, panel, ring))
    acts = gather.send(ring)
    partial = jnp.concatenate(partial, axis=0).reshape(-1, 2 * part, features)
    shares = exchange(partial, ("xl", "y", "xh"))
    shares = shares.reshape(2, -1, 2, 2, part, features).astype(jnp.float32)
    shares = jnp.sum(shares, axis=1).astype(jnp.bfloat16)
    shares = shares.transpose(2, 0, 1, 3, 4)
    input_grad = in_order(core, shares[:1], shares[1:], 0).reshape(-1, features)

    w_part = times(acts, panel, 0, 0)

    def piece(a, b):
        rows = w_part[a * features : (a + 1) * features]
        return lax.dynamic_slice_in_dim(rows, (far ^ b) * columns, columns, 1)

    w_grad = piece(0, 0)
    for a, b in PAIRS:
        w_grad = w_grad + to_partner(piece(a, b).astype(jnp.bfloat16), a, b)
    return (w_grad, input_grad)


def solution(mesh):
    rows, cols = mesh.devices.shape
    split = Mesh(
        mesh.devices.reshape(2, rows // 4, 2, cols // 2, 2), ("xl", "z", "core", "y", "xh")
    )
    row, col = ("xl", "z", "core"), ("y", "xh")
    return jax.shard_map(
        per_device,
        mesh=split,
        in_specs=(P(col, row), P(row, col), P(row, col)),
        out_specs=(P(row, col), P(col, row)),
        check_vma=False,
    )
```

```python
import jax
import jax.numpy as jnp
from jax import lax
from jax.sharding import Mesh, PartitionSpec as P

PAIRS = ((1, 0), (0, 1), (1, 1))


def swap(block, axis):
    return lax.ppermute(block, axis, ((0, 1), (1, 0)))


def to_partner(block, a, b):
    return lax.ppermute(block, ("xl", "xh"), [(i, i ^ (2 * a + b)) for i in range(4)])


def in_order(own, kept, got, axis):
    return jnp.concatenate(
        [jnp.where(own == 0, kept, got), jnp.where(own == 0, got, kept)], axis=axis
    )


def pick(block, index, axis):
    return lax.dynamic_slice_in_dim(block, index, 1, axis)


def exchange(pieces, axes):
    return lax.all_to_all(pieces, axes, split_axis=0, concat_axis=0, tiled=True)


def times(left, right, left_dim, right_dim):
    return lax.dot_general(
        left,
        right,
        (((left_dim,), (right_dim,)), ((), ())),
        preferred_element_type=jnp.float32,
    )


def ring_gather(block, axis):
    size = lax.axis_size(axis)
    me = lax.axis_index(axis)
    rows = block.shape[0]
    up = [(i, (i + 1) % size) for i in range(size)]
    down = [(i, (i - 1) % size) for i in range(size)]
    rising, falling = [block], [block]
    for _ in range(1, size // 2):
        rising.append(lax.ppermute(rising[-1], axis, up))
        falling.append(lax.ppermute(falling[-1], axis, down))
    rising, falling = yield rising, falling
    middle = rows // 2
    far = (
        lax.ppermute(rising[-1][:middle], axis, up),
        lax.ppermute(falling[-1][middle:], axis, down),
    )
    rising, falling, far = yield rising, falling, far
    blocks = falling[:] + list(far) + rising[:0:-1]
    panel = jnp.concatenate(blocks + blocks[:-1], axis=0)
    first = lax.rem(size - me, size) * rows
    yield lax.dynamic_slice_in_dim(panel, first, size * rows, 0)


def per_device(inputs, out_grad, weight):
    core = lax.axis_index("core")
    near = lax.axis_index("xl")
    far = lax.axis_index("xh")
    depth = lax.axis_size("z")
    tokens, columns = out_grad.shape
    features = inputs.shape[1]
    part = tokens // 4

    acts = inputs.reshape(2, 4, part, features)
    acts = jnp.concatenate([pick(acts, core, 0), pick(acts, 1 - core, 0)], axis=0)

    def quarter(a, b):
        return pick(acts, 2 * (near ^ a) + (far ^ b), 1).reshape(1, 2, part, features)

    came = {(a, b): to_partner(quarter(a, b), a, b) for a, b in PAIRS}
    came[0, 0] = quarter(0, 0)
    rows = [jnp.concatenate([came[0, b], came[1, b]], axis=3) for b in range(2)]
    acts = in_order(far, rows[0], rows[1], 0).reshape(4 * part, 2 * features)
    acts, out_grad, weight = lax.optimization_barrier((acts, out_grad, weight))

    grads = jnp.broadcast_to(
        out_grad.reshape(4, 1, part, columns), (4, depth, part, columns)
    ).reshape(-1, part, columns)
    grads = exchange(grads, ("xl", "xh", "z"))

    came = {(a, b): to_partner(weight, a, b) for a, b in PAIRS}
    came[0, 0] = weight
    weights = [in_order(far, came[a, 0], came[a, 1], 1) for a in range(2)]
    weights = in_order(near, weights[0], weights[1], 0)
    gather = ring_gather(acts, "y")
    ring = next(gather)
    grads, weights, ring = lax.optimization_barrier((grads, weights, ring))
    ring = gather.send(ring)

    panels = [
        g.reshape(2, 2, depth, 1, part, columns) for g in (grads, swap(grads, "core"))
    ]
    panels = [jnp.concatenate([g[:, 0], g[:, 1]], axis=4) for g in panels]
    panel = jnp.concatenate(panels, axis=2).reshape(-1, 2 * columns)
    partial = [
        times(panel, weights[i * features : (i + 1) * features], 1, 1).astype(jnp.bfloat16)
        for i in range(2)
    ]
    *partial, panel, ring = lax.optimization_barrier((*partial, panel, ring))
    acts = gather.send(ring)
    partial = jnp.concatenate(partial, axis=0).reshape(-1, 2 * part, features)
    shares = exchange(partial, ("xl", "y", "xh"))
    shares = shares.reshape(2, -1, 2, 2, part, features).astype(jnp.float32)
    shares = jnp.sum(shares, axis=1).astype(jnp.bfloat16)
    shares = shares.transpose(2, 0, 1, 3, 4)
    input_grad = in_order(core, shares[:1], shares[1:], 0).reshape(-1, features)

    w_part = times(acts, panel, 0, 0)

    def piece(a, b):
        rows = w_part[a * features : (a + 1) * features]
        return lax.dynamic_slice_in_dim(rows, (far ^ b) * columns, columns, 1)

    w_grad = piece(0, 0)
    for a, b in PAIRS:
        w_grad = w_grad + to_partner(piece(a, b).astype(jnp.bfloat16), a, b)
    return (w_grad, input_grad)


def solution(mesh):
    rows, cols = mesh.devices.shape
    split = Mesh(
        mesh.devices.reshape(2, rows // 4, 2, cols // 2, 2), ("xl", "z", "core", "y", "xh")
    )
    row, col = ("xl", "z", "core"), ("y", "xh")
    return jax.shard_map(
        per_device,
        mesh=split,
        in_specs=(P(col, row), P(row, col), P(row, col)),
        out_specs=(P(row, col), P(col, row)),
        check_vma=False,
    )
```

```python
import jax
import jax.numpy as jnp
from jax import lax
from jax.sharding import Mesh, PartitionSpec as P

PAIRS = ((1, 0), (0, 1), (1, 1))


def swap(block, axis):
    return lax.ppermute(block, axis, ((0, 1), (1, 0)))


def to_partner(block, a, b):
    return lax.ppermute(block, ("xl", "xh"), [(i, i ^ (2 * a + b)) for i in range(4)])


def in_order(own, kept, got, axis):
    return jnp.concatenate(
        [jnp.where(own == 0, kept, got), jnp.where(own == 0, got, kept)], axis=axis
    )


def pick(block, index, axis):
    return lax.dynamic_slice_in_dim(block, index, 1, axis)


def exchange(pieces, axes):
    return lax.all_to_all(pieces, axes, split_axis=0, concat_axis=0, tiled=True)


def times(left, right, left_dim, right_dim):
    return lax.dot_general(
        left,
        right,
        (((left_dim,), (right_dim,)), ((), ())),
        preferred_element_type=jnp.float32,
    )


def ring_gather(block, axis):
    size = lax.axis_size(axis)
    me = lax.axis_index(axis)
    rows = block.shape[0]
    up = [(i, (i + 1) % size) for i in range(size)]
    down = [(i, (i - 1) % size) for i in range(size)]
    rising, falling = [block], [block]
    for _ in range(1, size // 2):
        rising.append(lax.ppermute(rising[-1], axis, up))
        falling.append(lax.ppermute(falling[-1], axis, down))
    rising, falling = yield rising, falling
    far = lax.ppermute(rising[-1], axis, up)
    rising, falling, far = yield rising, falling, far
    blocks = falling + [far] + rising[:0:-1]
    panel = jnp.concatenate(blocks + blocks[:-1], axis=0)
    first = lax.rem(size - me, size) * rows
    yield lax.dynamic_slice_in_dim(panel, first, size * rows, 0)


def per_device(inputs, out_grad, weight):
    core = lax.axis_index("core")
    near = lax.axis_index("xl")
    far = lax.axis_index("xh")
    depth = lax.axis_size("z")
    tokens, columns = out_grad.shape
    features = inputs.shape[1]
    part = tokens // 4

    acts = inputs.reshape(2, 4, part, features)
    acts = jnp.concatenate([pick(acts, core, 0), pick(acts, 1 - core, 0)], axis=0)

    def quarter(a, b):
        return pick(acts, 2 * (near ^ a) + (far ^ b), 1).reshape(1, 2, part, features)

    came = {(a, b): to_partner(quarter(a, b), a, b) for a, b in PAIRS}
    came[0, 0] = quarter(0, 0)
    rows = [jnp.concatenate([came[0, b], came[1, b]], axis=3) for b in range(2)]
    acts = in_order(far, rows[0], rows[1], 0).reshape(4 * part, 2 * features)
    acts, out_grad, weight = lax.optimization_barrier((acts, out_grad, weight))

    grads = jnp.broadcast_to(
        out_grad.reshape(4, 1, part, columns), (4, depth, part, columns)
    ).reshape(-1, part, columns)
    grads = exchange(grads, ("xl", "xh", "z"))

    came = {(a, b): to_partner(weight, a, b) for a, b in PAIRS}
    came[0, 0] = weight
    gather = ring_gather(acts, "y")
    ring = next(gather)
    grads, came, ring = lax.optimization_barrier((grads, came, ring))
    ring = gather.send(ring)
    weights = [in_order(far, came[a, 0], came[a, 1], 1) for a in range(2)]
    weights = [
        jnp.where(near == 0, weights[0], weights[1]),
        jnp.where(near == 0, weights[1], weights[0]),
    ]

    panels = [
        g.reshape(2, 2, depth, 1, part, columns) for g in (grads, swap(grads, "core"))
    ]
    panels = [jnp.concatenate([g[:, 0], g[:, 1]], axis=4) for g in panels]
    panel = jnp.concatenate(panels, axis=2).reshape(-1, 2 * columns)
    partial = [times(panel, w, 1, 1).astype(jnp.bfloat16) for w in weights]
    *partial, panel, ring = lax.optimization_barrier((*partial, panel, ring))
    acts = gather.send(ring)
    partial = jnp.concatenate(partial, axis=0).reshape(-1, 2 * part, features)
    shares = exchange(partial, ("xl", "y", "xh"))
    shares = shares.reshape(2, -1, 2, 2, part, features).astype(jnp.float32)
    shares = jnp.sum(shares, axis=1).astype(jnp.bfloat16)
    shares = shares.transpose(2, 0, 1, 3, 4)
    input_grad = in_order(core, shares[:1], shares[1:], 0).reshape(-1, features)

    w_part = times(acts, panel, 0, 0)

    def piece(a, b):
        rows = w_part[a * features : (a + 1) * features]
        return lax.dynamic_slice_in_dim(rows, (far ^ b) * columns, columns, 1)

    w_grad = piece(0, 0)
    for a, b in PAIRS:
        w_grad = w_grad + to_partner(piece(a, b).astype(jnp.bfloat16), a, b)
    return (w_grad, input_grad)


def solution(mesh):
    rows, cols = mesh.devices.shape
    split = Mesh(
        mesh.devices.reshape(2, rows // 4, 2, cols // 2, 2), ("xl", "z", "core", "y", "xh")
    )
    row, col = ("xl", "z", "core"), ("y", "xh")
    return jax.shard_map(
        per_device,
        mesh=split,
        in_specs=(P(col, row), P(row, col), P(row, col)),
        out_specs=(P(row, col), P(col, row)),
        check_vma=False,
    )
```

```python
import jax
import jax.numpy as jnp
from jax import lax
from jax.sharding import Mesh, PartitionSpec as P

PAIRS = ((1, 0), (0, 1), (1, 1))


def swap(block, axis):
    return lax.ppermute(block, axis, ((0, 1), (1, 0)))


def to_partner(block, a, b):
    return lax.ppermute(block, ("xl", "xh"), [(i, i ^ (2 * a + b)) for i in range(4)])


def in_order(own, kept, got, axis):
    return jnp.concatenate(
        [jnp.where(own == 0, kept, got), jnp.where(own == 0, got, kept)], axis=axis
    )


def pick(block, index, axis):
    return lax.dynamic_slice_in_dim(block, index, 1, axis)


def exchange(pieces, axes):
    return lax.all_to_all(pieces, axes, split_axis=0, concat_axis=0, tiled=True)


def times(left, right, left_dim, right_dim):
    return lax.dot_general(
        left,
        right,
        (((left_dim,), (right_dim,)), ((), ())),
        preferred_element_type=jnp.float32,
    )


def ring_gather(block, axis):
    size = lax.axis_size(axis)
    me = lax.axis_index(axis)
    rows = block.shape[0]
    up = [(i, (i + 1) % size) for i in range(size)]
    down = [(i, (i - 1) % size) for i in range(size)]
    rising, falling = [block], [block]
    for _ in range(1, size // 2):
        rising.append(lax.ppermute(rising[-1], axis, up))
        falling.append(lax.ppermute(falling[-1], axis, down))
    rising, falling = yield rising, falling
    far = lax.ppermute(rising[-1], axis, up)
    rising, falling, far = yield rising, falling, far
    blocks = falling + [far] + rising[:0:-1]
    panel = jnp.concatenate(blocks + blocks[:-1], axis=0)
    first = lax.rem(size - me, size) * rows
    yield lax.dynamic_slice_in_dim(panel, first, size * rows, 0)


def per_device(inputs, out_grad, weight):
    core = lax.axis_index("core")
    near = lax.axis_index("xl")
    far = lax.axis_index("xh")
    depth = lax.axis_size("z")
    tokens, columns = out_grad.shape
    features = inputs.shape[1]
    part = tokens // 4

    grads = jnp.broadcast_to(
        out_grad.reshape(4, 1, part, columns), (4, depth, part, columns)
    ).reshape(-1, part, columns)
    grads = exchange(grads, ("xl", "xh", "z"))

    acts = inputs.reshape(2, 4, part, features)
    acts = jnp.concatenate([pick(acts, core, 0), pick(acts, 1 - core, 0)], axis=0)

    def quarter(a, b):
        return pick(acts, 2 * (near ^ a) + (far ^ b), 1).reshape(1, 2, part, features)

    came = {(a, b): to_partner(quarter(a, b), a, b) for a, b in PAIRS}
    came[0, 0] = quarter(0, 0)
    rows = [jnp.concatenate([came[0, b], came[1, b]], axis=3) for b in range(2)]
    acts = in_order(far, rows[0], rows[1], 0).reshape(4 * part, 2 * features)
    acts, weight = lax.optimization_barrier((acts, weight))

    came = {(a, b): to_partner(weight, a, b) for a, b in PAIRS}
    came[0, 0] = weight
    gather = ring_gather(acts, "y")
    ring = next(gather)
    grads, came, ring = lax.optimization_barrier((grads, came, ring))
    ring = gather.send(ring)
    weights = [in_order(far, came[a, 0], came[a, 1], 1) for a in range(2)]
    weights = [
        jnp.where(near == 0, weights[0], weights[1]),
        jnp.where(near == 0, weights[1], weights[0]),
    ]

    panels = [
        g.reshape(2, 2, depth, 1, part, columns) for g in (grads, swap(grads, "core"))
    ]
    panels = [jnp.concatenate([g[:, 0], g[:, 1]], axis=4) for g in panels]
    panel = jnp.concatenate(panels, axis=2).reshape(-1, 2 * columns)
    partial = [times(panel, w, 1, 1).astype(jnp.bfloat16) for w in weights]
    *partial, panel, ring = lax.optimization_barrier((*partial, panel, ring))
    acts = gather.send(ring)
    partial = jnp.concatenate(partial, axis=0).reshape(-1, 2 * part, features)
    shares = exchange(partial, ("xl", "y", "xh"))
    shares = shares.reshape(2, -1, 2, 2, part, features).astype(jnp.float32)
    shares = jnp.sum(shares, axis=1).astype(jnp.bfloat16)
    shares = shares.transpose(2, 0, 1, 3, 4)
    input_grad = in_order(core, shares[:1], shares[1:], 0).reshape(-1, features)

    w_part = times(acts, panel, 0, 0)

    def piece(a, b):
        rows = w_part[a * features : (a + 1) * features]
        return lax.dynamic_slice_in_dim(rows, (far ^ b) * columns, columns, 1)

    w_grad = piece(0, 0)
    for a, b in PAIRS:
        w_grad = w_grad + to_partner(piece(a, b).astype(jnp.bfloat16), a, b)
    return (w_grad, input_grad)


def solution(mesh):
    rows, cols = mesh.devices.shape
    split = Mesh(
        mesh.devices.reshape(2, rows // 4, 2, cols // 2, 2), ("xl", "z", "core", "y", "xh")
    )
    row, col = ("xl", "z", "core"), ("y", "xh")
    return jax.shard_map(
        per_device,
        mesh=split,
        in_specs=(P(col, row), P(row, col), P(row, col)),
        out_specs=(P(row, col), P(col, row)),
        check_vma=False,
    )
```

```python
import jax
import jax.numpy as jnp
from jax import lax
from jax.sharding import Mesh, PartitionSpec as P

PAIRS = ((1, 0), (0, 1), (1, 1))


def swap(block, axis):
    return lax.ppermute(block, axis, ((0, 1), (1, 0)))


def to_partner(block, a, b):
    return lax.ppermute(block, ("xl", "xh"), [(i, i ^ (2 * a + b)) for i in range(4)])


def in_order(own, kept, got, axis):
    return jnp.concatenate(
        [jnp.where(own == 0, kept, got), jnp.where(own == 0, got, kept)], axis=axis
    )


def pick(block, index, axis):
    return lax.dynamic_slice_in_dim(block, index, 1, axis)


def exchange(pieces, axes):
    return lax.all_to_all(pieces, axes, split_axis=0, concat_axis=0, tiled=True)


def times(left, right, left_dim, right_dim):
    return lax.dot_general(
        left,
        right,
        (((left_dim,), (right_dim,)), ((), ())),
        preferred_element_type=jnp.float32,
    )


def ring_gather(block, axis):
    size = lax.axis_size(axis)
    me = lax.axis_index(axis)
    rows = block.shape[0]
    up = [(i, (i + 1) % size) for i in range(size)]
    down = [(i, (i - 1) % size) for i in range(size)]
    rising, falling = [block], [block]
    for _ in range(1, size // 2):
        rising.append(lax.ppermute(rising[-1], axis, up))
        falling.append(lax.ppermute(falling[-1], axis, down))
    rising, falling = yield rising, falling
    far = lax.ppermute(rising[-1], axis, up)
    rising, falling, far = yield rising, falling, far
    blocks = falling + [far] + rising[:0:-1]
    panel = jnp.concatenate(blocks + blocks[:-1], axis=0)
    first = lax.rem(size - me, size) * rows
    yield lax.dynamic_slice_in_dim(panel, first, size * rows, 0)


def per_device(inputs, out_grad, weight):
    core = lax.axis_index("core")
    near = lax.axis_index("xl")
    far = lax.axis_index("xh")
    depth = lax.axis_size("z")
    tokens, columns = out_grad.shape
    features = inputs.shape[1]
    part = tokens // 4

    grads = jnp.broadcast_to(
        out_grad.reshape(4, 1, part, columns), (4, depth, part, columns)
    ).reshape(-1, part, columns)
    grads = exchange(grads, ("xl", "xh", "z"))

    acts = inputs.reshape(2, 4, part, features)
    acts = jnp.concatenate([pick(acts, core, 0), pick(acts, 1 - core, 0)], axis=0)

    def quarter(a, b):
        return pick(acts, 2 * (near ^ a) + (far ^ b), 1).reshape(1, 2, part, features)

    came = {(a, b): to_partner(quarter(a, b), a, b) for a, b in PAIRS}
    came[0, 0] = quarter(0, 0)
    rows = [jnp.concatenate([came[0, b], came[1, b]], axis=3) for b in range(2)]
    acts = in_order(far, rows[0], rows[1], 0).reshape(4 * part, 2 * features)
    weight = in_order(far, weight, swap(weight, "xh"), 1)
    acts, weight = lax.optimization_barrier((acts, weight))

    partner = swap(weight, "xl")
    gather = ring_gather(acts, "y")
    ring = next(gather)
    grads, weight, partner, ring = lax.optimization_barrier((grads, weight, partner, ring))
    ring = gather.send(ring)
    weights = [
        jnp.where(near == 0, weight, partner),
        jnp.where(near == 0, partner, weight),
    ]

    panels = [
        g.reshape(2, 2, depth, 1, part, columns) for g in (grads, swap(grads, "core"))
    ]
    panels = [jnp.concatenate([g[:, 0], g[:, 1]], axis=4) for g in panels]
    panel = jnp.concatenate(panels, axis=2).reshape(-1, 2 * columns)
    partial = [times(panel, w, 1, 1).astype(jnp.bfloat16) for w in weights]
    *partial, panel, ring = lax.optimization_barrier((*partial, panel, ring))
    acts = gather.send(ring)
    partial = jnp.concatenate(partial, axis=0).reshape(-1, 2 * part, features)
    shares = exchange(partial, ("xl", "y", "xh"))
    shares = shares.reshape(2, -1, 2, 2, part, features).astype(jnp.float32)
    shares = jnp.sum(shares, axis=1).astype(jnp.bfloat16)
    shares = shares.transpose(2, 0, 1, 3, 4)
    input_grad = in_order(core, shares[:1], shares[1:], 0).reshape(-1, features)

    w_part = times(acts, panel, 0, 0)

    def piece(a, b):
        rows = w_part[a * features : (a + 1) * features]
        return lax.dynamic_slice_in_dim(rows, (far ^ b) * columns, columns, 1)

    w_grad = piece(0, 0)
    for a, b in PAIRS:
        w_grad = w_grad + to_partner(piece(a, b).astype(jnp.bfloat16), a, b)
    return (w_grad, input_grad)


def solution(mesh):
    rows, cols = mesh.devices.shape
    split = Mesh(
        mesh.devices.reshape(2, rows // 4, 2, cols // 2, 2), ("xl", "z", "core", "y", "xh")
    )
    row, col = ("xl", "z", "core"), ("y", "xh")
    return jax.shard_map(
        per_device,
        mesh=split,
        in_specs=(P(col, row), P(row, col), P(row, col)),
        out_specs=(P(row, col), P(col, row)),
        check_vma=False,
    )
```

```python
import jax
import jax.numpy as jnp
from jax import lax
from jax.sharding import Mesh, PartitionSpec as P

PAIRS = ((1, 0), (0, 1), (1, 1))


def swap(block, axis):
    return lax.ppermute(block, axis, ((0, 1), (1, 0)))


def to_partner(block, a, b):
    return lax.ppermute(block, ("xl", "xh"), [(i, i ^ (2 * a + b)) for i in range(4)])


def in_order(own, kept, got, axis):
    return jnp.concatenate(
        [jnp.where(own == 0, kept, got), jnp.where(own == 0, got, kept)], axis=axis
    )


def pick(block, index, axis):
    return lax.dynamic_slice_in_dim(block, index, 1, axis)


def exchange(pieces, axes):
    return lax.all_to_all(pieces, axes, split_axis=0, concat_axis=0, tiled=True)


def times(left, right, left_dim, right_dim):
    return lax.dot_general(
        left,
        right,
        (((left_dim,), (right_dim,)), ((), ())),
        preferred_element_type=jnp.float32,
    )


def ring_gather(block, axis):
    size = lax.axis_size(axis)
    me = lax.axis_index(axis)
    rows = block.shape[0]
    up = [(i, (i + 1) % size) for i in range(size)]
    down = [(i, (i - 1) % size) for i in range(size)]
    rising, falling = [block], [block]
    for _ in range(1, size // 2):
        rising.append(lax.ppermute(rising[-1], axis, up))
        falling.append(lax.ppermute(falling[-1], axis, down))
    rising, falling = yield rising, falling
    middle = rows // 2
    far = (
        lax.ppermute(rising[-1][:middle], axis, up),
        lax.ppermute(falling[-1][middle:], axis, down),
    )
    rising, falling, far = yield rising, falling, far
    blocks = falling + list(far) + rising[:0:-1]
    panel = jnp.concatenate(blocks + blocks[:-1], axis=0)
    first = lax.rem(size - me, size) * rows
    yield lax.dynamic_slice_in_dim(panel, first, size * rows, 0)


def per_device(inputs, out_grad, weight):
    core = lax.axis_index("core")
    near = lax.axis_index("xl")
    far = lax.axis_index("xh")
    depth = lax.axis_size("z")
    tokens, columns = out_grad.shape
    features = inputs.shape[1]
    part = tokens // 4

    grads = jnp.broadcast_to(
        out_grad.reshape(4, 1, part, columns), (4, depth, part, columns)
    ).reshape(-1, part, columns)
    grads = exchange(grads, ("xl", "xh", "z"))

    acts = inputs.reshape(2, 4, part, features)
    acts = jnp.concatenate([pick(acts, core, 0), pick(acts, 1 - core, 0)], axis=0)

    def quarter(a, b):
        return pick(acts, 2 * (near ^ a) + (far ^ b), 1).reshape(1, 2, part, features)

    came = {(a, b): to_partner(quarter(a, b), a, b) for a, b in PAIRS}
    came[0, 0] = quarter(0, 0)
    rows = [jnp.concatenate([came[0, b], came[1, b]], axis=3) for b in range(2)]
    acts = in_order(far, rows[0], rows[1], 0).reshape(4 * part, 2 * features)
    acts, weight = lax.optimization_barrier((acts, weight))

    came = {(a, b): to_partner(weight, a, b) for a, b in PAIRS}
    came[0, 0] = weight
    gather = ring_gather(acts, "y")
    ring = next(gather)
    grads, came, ring = lax.optimization_barrier((grads, came, ring))
    ring = gather.send(ring)
    weights = [in_order(far, came[a, 0], came[a, 1], 1) for a in range(2)]
    weights = [
        jnp.where(near == 0, weights[0], weights[1]),
        jnp.where(near == 0, weights[1], weights[0]),
    ]

    panels = [
        g.reshape(2, 2, depth, 1, part, columns) for g in (grads, swap(grads, "core"))
    ]
    panels = [jnp.concatenate([g[:, 0], g[:, 1]], axis=4) for g in panels]
    panel = jnp.concatenate(panels, axis=2).reshape(-1, 2 * columns)
    partial = [times(panel, w, 1, 1).astype(jnp.bfloat16) for w in weights]
    *partial, panel, ring = lax.optimization_barrier((*partial, panel, ring))
    acts = gather.send(ring)
    partial = jnp.concatenate(partial, axis=0).reshape(-1, 2 * part, features)
    shares = exchange(partial, ("xl", "y", "xh"))
    shares = shares.reshape(2, -1, 2, 2, part, features).astype(jnp.float32)
    shares = jnp.sum(shares, axis=1).astype(jnp.bfloat16)
    shares = shares.transpose(2, 0, 1, 3, 4)
    input_grad = in_order(core, shares[:1], shares[1:], 0).reshape(-1, features)

    w_part = times(acts, panel, 0, 0)

    def piece(a, b):
        rows = w_part[a * features : (a + 1) * features]
        return lax.dynamic_slice_in_dim(rows, (far ^ b) * columns, columns, 1)

    w_grad = piece(0, 0)
    for a, b in PAIRS:
        w_grad = w_grad + to_partner(piece(a, b).astype(jnp.bfloat16), a, b)
    return (w_grad, input_grad)


def solution(mesh):
    rows, cols = mesh.devices.shape
    split = Mesh(
        mesh.devices.reshape(2, rows // 4, 2, cols // 2, 2), ("xl", "z", "core", "y", "xh")
    )
    row, col = ("xl", "z", "core"), ("y", "xh")
    return jax.shard_map(
        per_device,
        mesh=split,
        in_specs=(P(col, row), P(row, col), P(row, col)),
        out_specs=(P(row, col), P(col, row)),
        check_vma=False,
    )
```
